512 devices in a mesh: dp: 128 (over z, x_hi, y), sub: 4 (over x_lo, core).
Axes of the slice: x: 4 (x_hi: 2, x_lo: 2; x = x_hi * 2 + x_lo), y: 8, z: 8, core: 2. Of those that a mesh axis runs over, the one named last changes fastest.
Arguments:
- queries: bfloat16 [65536, 3584], P(('dp', 'sub')), may hold values from -4 to 4
- passages: bfloat16 [65536, 3584], P(('dp', 'sub')), may hold values from -4 to 4
- requests: int32 [512, 128, 3], P(('dp', 'sub')), may hold values from 0 to 127, as said below
- counts: int32 [512, 128], P(('dp', 'sub')), may hold values from 1 to 3, as said below
- neg_slot: int32 [65536, 7], P(('dp', 'sub')), may hold values from 0 to 383, as said below
Outputs:
- question_derivative: bfloat16 [65536, 3584], P(('dp', 'sub'))
- passage_grad: bfloat16 [65536, 3584], P(('dp', 'sub'))
- loss: float32 [], replicated
The draws below stay inside these ranges and needn't reach their ends.
Inputs may be any that keep to these rules, and one draw needn't show every extreme that they name: `requests`: rows asked of an owner, inside that owner's block. Slots c < counts[d, o] of owner o are live for device d. `neg_slot`: each row names 7 different live slots of its own device's table, slot t belonging to owner t // 3 and position t % 3.
All inputs are finite; a program needn't handle non-finite values.
Results may differ from the reference program's by a relative error of at most 0.0062.
Values may be sent and summed in bfloat16 or wider, within the bound.
A program may use at most 128 MiB of HBM per device.

```python
import math
import jax
import jax.numpy as jnp
from jax import lax

D = 3584
ROWS = 128
SHIFTS = 4
NEG = 7
CAP = 3
DEVS = 512
NQ = 65536
SLOTS = 384
N_DP = 128
N_SUB = 4


positive_mix = 0.15


neighbour_mix = 0.1


negative_mix = 0.1


noise_mix = 0.94


def owner_loads(key):
    key = jax.random.fold_in(key, 101)
    first, second = jax.random.split(key)
    owners = SLOTS // CAP
    base = jax.random.randint(first, (DEVS, owners), 1, CAP + 1)
    heavy = jax.random.permutation(second, owners)[:max(1, owners // 8)]
    owner_ids = jnp.arange(owners, dtype=jnp.int32)
    is_heavy = jnp.any(owner_ids[:, None] == heavy[None, :], axis=1)
    is_heavy = jnp.logical_or(is_heavy, owner_ids == owners - 1)
    return jnp.where(is_heavy[None, :], CAP, base).astype(jnp.int32)


def request_table(key):
    key = jax.random.fold_in(key, 12)
    return jax.random.randint(key, (DEVS, SLOTS // CAP, CAP), 0, ROWS).astype(jnp.int32)


def negative_table(key):
    loads = owner_loads(key)
    key = jax.random.fold_in(key, 13)
    slot_ids = jnp.arange(SLOTS, dtype=jnp.int32)
    row_ids = jnp.arange(ROWS, dtype=jnp.int32)
    live_slot = slot_ids[None, :] % CAP < jnp.repeat(loads, CAP, axis=1)
    scores = jax.random.randint(key, (DEVS, ROWS, SLOTS), 0, 2 ** 20) * SLOTS + slot_ids[None, None, :]
    end_slot = jnp.logical_or(slot_ids == 0, slot_ids == SLOTS - 1)
    forced = jnp.logical_and(row_ids[:, None] == 0, end_slot[None, :])
    scores = jnp.where(forced[None, :, :], 2 ** 30 + slot_ids[None, None, :], scores)
    scores = jnp.where(live_slot[:, None, :], scores, -1 - slot_ids[None, None, :])
    picked = jax.lax.top_k(scores, NEG)[1]
    return picked.reshape(DEVS * ROWS, NEG).astype(jnp.int32)


def base_rows(key, row_ids):
    base_key = jax.random.fold_in(key, 201)

    def one_row(row):
        return jnp.clip(jax.random.normal(jax.random.fold_in(base_key, row), (D,), jnp.float32), -3.0, 3.0)
    return jax.vmap(one_row)(row_ids)


def column_scales(key, spread):
    key = jax.random.fold_in(key, 202)
    return jnp.exp(jax.random.uniform(key, (D,), jnp.float32, -spread, spread))


def finish_rows(values, scales, scale_key, lowest, highest):
    row_scale = jnp.exp(jax.random.uniform(scale_key, (NQ, 1), jnp.float32, math.log(lowest), math.log(highest)))
    values = values * scales[None, :] * row_scale * (1.0 / math.sqrt(D))
    return jnp.clip(values, -4.0, 4.0).astype(jnp.bfloat16)


def draw_counts(key, part):
    loads = owner_loads(key)
    return loads


def draw_requests(key, part):
    tables = request_table(key)
    return tables


def draw_neg_slot(key, part):
    picked = negative_table(key)
    return picked


def draw_passages(key, part):
    spread, lowest, highest = (1.15, 0.4, 4.0)
    scales = column_scales(key, spread)
    values = base_rows(key, jnp.arange(NQ, dtype=jnp.int32))
    key = jax.random.fold_in(key, 22)
    return finish_rows(values, scales, key, lowest, highest)


def draw_queries(key, part):
    spread, lowest, highest = (1.15, 0.4, 4.0)
    scales = column_scales(key, spread)
    tables = request_table(key)
    negatives = negative_table(key).reshape(DEVS, ROWS, NEG)
    source = key
    key = jax.random.fold_in(key, 21)
    noise_key, scale_key = jax.random.split(key)
    row_ids = jnp.arange(ROWS, dtype=jnp.int32)

    def one_device(device):
        dp_index = device // N_SUB
        sub_index = device % N_SUB
        total = positive_mix * base_rows(source, device * ROWS + row_ids)
        for offset in range(1, SHIFTS):
            document_section = (dp_index - offset) % N_DP * N_SUB + sub_index
            total = total + neighbour_mix * base_rows(source, document_section * ROWS + row_ids)
        flat_table = tables[device].reshape(SLOTS)
        for column in range(NEG):
            slot_ids = negatives[device][:, column]
            global_row = (slot_ids // CAP * N_SUB + sub_index) * ROWS + flat_table[slot_ids]
            total = total + negative_mix * base_rows(source, global_row)
        noise = jnp.clip(jax.random.normal(jax.random.fold_in(noise_key, device), (ROWS, D), jnp.float32), -3.0, 3.0)
        total = total + noise_mix * noise
        return total
    values = jax.lax.map(one_device, jnp.arange(DEVS, dtype=jnp.int32)).reshape(NQ, D)
    return finish_rows(values, scales, scale_key, lowest, highest)


def setup_inputs(seed: int = 0) -> dict:
    arg_keys = jax.random.split(jax.random.key(seed), 6)
    queries = draw_queries(jax.random.fold_in(arg_keys[5], 71), 0)
    passages = draw_passages(jax.random.fold_in(arg_keys[5], 71), 0)
    requests = draw_requests(jax.random.fold_in(arg_keys[5], 71), 0)
    counts = draw_counts(jax.random.fold_in(arg_keys[5], 71), 0)
    neg_slot = draw_neg_slot(jax.random.fold_in(arg_keys[5], 71), 0)
    return {"queries": queries, "passages": passages, "requests": requests, "counts": counts, "neg_slot": neg_slot}


SHARPNESS_FACTOR = 50.0
EPSILON = 1e-06

def unit_rows(values):
    widened = values.astype(jnp.float32)
    lengths = jnp.sqrt(lax.optimization_barrier(jnp.sum(widened * widened, axis=1, keepdims=True)) + EPSILON)
    return (widened / lengths, lengths)

def project_back(grad, unit, lengths):
    radial = lax.optimization_barrier(jnp.sum(unit * grad, axis=1, keepdims=True))
    return ((grad - unit * radial) / lengths).astype(jnp.bfloat16)

def reference(queries, passages, requests, counts, neg_slot):
    query_unit, query_len = unit_rows(queries)
    passage_unit, passage_len = unit_rows(passages)
    query_blocks = query_unit.astype(jnp.bfloat16).reshape(N_DP, N_SUB, ROWS, D)
    passage_blocks = passage_unit.astype(jnp.bfloat16).reshape(N_DP, N_SUB, ROWS, D)
    neg_blocks = neg_slot.reshape(N_DP, N_SUB, ROWS, NEG)
    asked_table = requests.reshape(N_DP, N_SUB, N_DP, CAP)
    count_table = counts.reshape(N_DP, N_SUB, N_DP)
    slot_ids = jnp.arange(N_DP * CAP, dtype=jnp.int32)
    owner_ids = slot_ids // CAP
    identity = jnp.eye(ROWS, dtype=jnp.float32)

    def device_step(carried, device_index):
        normalized_document_derivative, aggregate_objective = carried
        dp_index = device_index // N_SUB
        sub_index = device_index % N_SUB
        question_reduced_precision = query_blocks[dp_index, sub_index]
        section_sequence = [passage_blocks[(dp_index - offset) % N_DP, sub_index] for offset in range(SHIFTS)]
        wanted_rows = asked_table[dp_index, sub_index].reshape(N_DP * CAP)
        retrieved_distractors = passage_blocks[owner_ids, sub_index, wanted_rows]
        live_slot = slot_ids % CAP < count_table[dp_index, sub_index][owner_ids]
        chosen = lax.optimization_barrier(jnp.sum((neg_blocks[dp_index, sub_index][:, :, None] == slot_ids[None, None, :]).astype(jnp.float32), axis=1))
        distractor_indicator = chosen * live_slot.astype(jnp.float32)[None, :]
        section_similarity_scores = [SHARPNESS_FACTOR * jnp.dot(question_reduced_precision, document_section.T, preferred_element_type=jnp.float32) for document_section in section_sequence]
        powers = [jnp.exp(logit) for logit in section_similarity_scores]
        distractor_exponentials = jnp.exp(SHARPNESS_FACTOR * jnp.dot(question_reduced_precision, retrieved_distractors.T, preferred_element_type=jnp.float32)) * distractor_indicator
        totals = lax.optimization_barrier(jnp.sum(distractor_exponentials, axis=1))
        for power in powers:
            totals = totals + lax.optimization_barrier(jnp.sum(power, axis=1))
        aggregate_objective = aggregate_objective + jnp.sum(jnp.log(totals) - jnp.diagonal(section_similarity_scores[0]))
        distractor_importance = (distractor_exponentials / totals[:, None]).astype(jnp.bfloat16)
        question_derivative = jnp.dot(distractor_importance, retrieved_distractors, preferred_element_type=jnp.float32)
        for offset in range(SHIFTS):
            normalized_probabilities = powers[offset] / totals[:, None]
            if offset == 0:
                normalized_probabilities = normalized_probabilities - identity
            normalized_probabilities = normalized_probabilities.astype(jnp.bfloat16)
            question_derivative = question_derivative + jnp.dot(normalized_probabilities, section_sequence[offset], preferred_element_type=jnp.float32)
            section_objective_piece = SHARPNESS_FACTOR * jnp.dot(normalized_probabilities.T, question_reduced_precision, preferred_element_type=jnp.float32)
            normalized_document_derivative = normalized_document_derivative.at[(dp_index - offset) % N_DP * N_SUB + sub_index].add(section_objective_piece)
        position_aggregates = (SHARPNESS_FACTOR * jnp.dot(distractor_importance.T, question_reduced_precision, preferred_element_type=jnp.float32)).astype(jnp.bfloat16)
        normalized_document_derivative = normalized_document_derivative.at[owner_ids * N_SUB + sub_index, wanted_rows].add(position_aggregates.astype(jnp.float32))
        return ((normalized_document_derivative, aggregate_objective), SHARPNESS_FACTOR * question_derivative)
    start = (jnp.zeros((N_DP * N_SUB, ROWS, D), jnp.float32), jnp.zeros((), jnp.float32))
    (normalized_document_derivative, aggregate_objective), unit_qgrad = lax.scan(device_step, start, jnp.arange(N_DP * N_SUB, dtype=jnp.int32))
    question_derivative = project_back(unit_qgrad.reshape(NQ, D), query_unit, query_len)
    passage_grad = project_back(normalized_document_derivative.reshape(NQ, D), passage_unit, passage_len)
    return (question_derivative, passage_grad, aggregate_objective / NQ)
```

```python
import functools

import jax
import jax.numpy as jnp
import numpy as np
from jax import lax
from jax.experimental import pallas as pl
from jax.experimental.pallas import tpu as pltpu
from jax.sharding import PartitionSpec as P

SHIFTS = 4
CAP = 3
SHARPNESS = 50.0
EPSILON = 1e-06
Z_SIZE = 8
TILE = 256
MESH = pl.DeviceIdType.MESH
F32 = jnp.float32
BF16 = jnp.bfloat16


def tables(nz, nw):
    slots = nz * nw * CAP
    z, w, c = np.meshgrid(np.arange(nz), np.arange(nw), np.arange(CAP), indexing="ij")
    slot = ((z * nw + w) * CAP + c).reshape(-1)
    to_w = np.zeros((2 * slots, 2 * slots), np.float32)
    to_z = np.zeros((2 * slots, 2 * slots), np.float32)
    for half in range(2):
        by_w = (((w * 2 + half) * nz + z) * CAP + c).reshape(-1)
        by_z = (((z * 2 + half) * nw + w) * CAP + c).reshape(-1)
        to_w[by_w, half * slots + slot] = 1
        to_z[by_z, by_w] = 1
    expand = np.zeros((slots, nz * nw), np.float32)
    expand[slot, (w * nz + z).reshape(-1)] = 1
    column = np.zeros((slots, 128), np.float32)
    column[slot, c.reshape(-1)] = 1
    swap = np.zeros((nz * nw, nz * nw), np.float32)
    zz, ww = np.meshgrid(np.arange(nz), np.arange(nw), indexing="ij")
    swap[(ww * nz + zz).reshape(-1), (zz * nw + ww).reshape(-1)] = 1
    spread = np.zeros((nz * nw, slots), np.float32)
    spread[slot // CAP, slot] = 1
    place = np.broadcast_to((np.arange(slots) % CAP).astype(np.float32), (8, slots))
    b = lambda v: jnp.asarray(np.ascontiguousarray(v), BF16)
    return (
        b(to_w),
        b(to_w.T),
        b(to_z),
        b(expand),
        jnp.asarray(column),
        b(swap),
        b(spread),
        jnp.asarray(np.ascontiguousarray(place)),
    )


def mm(a, b):
    return jnp.dot(a, b, preferred_element_type=F32)


def mm_nt(a, b):
    return lax.dot_general(a, b, (((1,), (1,)), ((), ())), preferred_element_type=F32)


def at(index, size):
    return pl.ds(pl.multiple_of(index * size, size), size)


class Exchange:
    def __init__(self, place, x, y, bufs, sems, to_w, to_w_t, to_z):
        self.nz, self.nw, self.z, self.w, self.sub = place
        self.x, self.y = x, y
        self.r0, self.w0, self.rw0, self.w1, self.r1, self.z1 = bufs
        self.zs, self.zr, self.ws, self.wr, self.ls = sems
        self.to_w, self.to_w_t, self.to_z = to_w, to_w_t, to_z
        self.half = x.shape[1] // 2
        self.quarter = self.half // 2
        self.slots = x.shape[0]
        self.zrows = self.nw * CAP
        self.wrows = 2 * self.nz * CAP

    def z_peer(self, k):
        return lax.rem(self.z + k, self.nz)

    def w_peer(self, k):
        return lax.rem(self.w + k, self.nw)

    def z_dev(self, t):
        return (t * self.nw + self.w, self.sub)

    def w_dev(self, t):
        return (self.z * self.nw + t, self.sub)

    def z0(self, to, frm):
        return pltpu.make_async_remote_copy(
            self.x.at[at(to, self.zrows), pl.ds(0, self.half)],
            self.r0.at[at(frm, self.zrows)],
            self.zs.at[0, to],
            self.zr.at[0, frm],
            device_id=self.z_dev(to),
            device_id_type=MESH,
        )

    def z1c(self, h, to, frm):
        rows = pl.ds(pl.multiple_of(to * 2 * self.zrows + h * self.zrows, self.zrows), self.zrows)
        return pltpu.make_async_remote_copy(
            self.z1.at[rows],
            self.y.at[at(frm, self.zrows), pl.ds(self.half + h * self.quarter, self.quarter)],
            self.zs.at[1 + h, to],
            self.zr.at[1 + h, frm],
            device_id=self.z_dev(to),
            device_id_type=MESH,
        )

    def wc(self, kind, to, frm):
        src, dst = ((self.w0, self.rw0), (self.w1, self.r1))[kind]
        return pltpu.make_async_remote_copy(
            src.at[at(to, self.wrows)],
            dst.at[at(frm, self.wrows)],
            self.ws.at[kind, to],
            self.wr.at[kind, frm],
            device_id=self.w_dev(to),
            device_id_type=MESH,
        )

    def own(self, which):
        if which == 0:
            return pltpu.make_async_copy(
                self.x.at[at(self.z, self.zrows), pl.ds(0, self.half)],
                self.r0.at[at(self.z, self.zrows)],
                self.ls.at[0],
            )
        if which in (1, 2):
            src, dst = ((self.w0, self.rw0), (self.w1, self.r1))[which - 1]
            return pltpu.make_async_copy(
                src.at[at(self.w, self.wrows)], dst.at[at(self.w, self.wrows)], self.ls.at[which]
            )
        h = which - 3
        rows = pl.ds(
            pl.multiple_of(self.z * 2 * self.zrows + h * self.zrows, self.zrows), self.zrows
        )
        return pltpu.make_async_copy(
            self.z1.at[rows],
            self.y.at[at(self.z, self.zrows), pl.ds(self.half + h * self.quarter, self.quarter)],
            self.ls.at[which],
        )

    def each_z(self, act):
        lax.fori_loop(1, self.nz, lambda k, n: (act(self.z_peer(k)), n)[1], 0)

    def each_w(self, act):
        lax.fori_loop(1, self.nw, lambda k, n: (act(self.w_peer(k)), n)[1], 0)

    def reorder_to_w(self, dst, src, first):
        step = self.slots // 2 if self.slots % 32 == 0 else self.slots
        left = src[:, pl.ds(first, self.quarter)]
        right = src[:, pl.ds(first + self.quarter, self.quarter)]

        def body(i, n):
            m = self.to_w.at[at(i, step)]
            dst[at(i, step), :] = (
                mm(m[:, pl.ds(0, self.slots)], left)
                + mm(m[:, pl.ds(self.slots, self.slots)], right)
            ).astype(BF16)
            return n

        lax.fori_loop(0, 2 * self.slots // step, body, 0)

    def start_left(self):
        self.each_z(lambda t: self.z0(t, self.z).start())
        self.own(0).start()

    def start_right(self):
        self.reorder_to_w(self.w1, self.x, self.half)
        self.each_w(lambda t: self.wc(1, t, self.w).start())
        self.own(2).start()

    def turn_left(self):
        self.own(0).wait()
        self.each_z(lambda t: self.z0(self.z, t).wait_recv())
        self.reorder_to_w(self.w0, self.r0, 0)
        self.each_w(lambda t: self.wc(0, t, self.w).start())
        self.own(1).start()

    def turn_right(self):
        self.own(2).wait()
        self.each_w(lambda t: self.wc(1, self.w, t).wait_recv())
        step = self.slots // 2 if self.slots % 32 == 0 else self.slots

        def body(i, n):
            self.z1[at(i, step), :] = mm(self.to_z[at(i, step), :], self.r1[...]).astype(BF16)
            return n

        lax.fori_loop(0, 2 * self.slots // step, body, 0)
        for h in range(2):
            self.each_z(lambda t: self.z1c(h, t, self.z).start())
            self.own(3 + h).start()

    def end_left(self):
        self.own(1).wait()
        self.each_w(lambda t: self.wc(0, self.w, t).wait_recv())
        for h in range(2):
            self.y[:, pl.ds(h * self.quarter, self.quarter)] = mm(
                self.to_w_t[pl.ds(h * self.slots, self.slots), :], self.rw0[...]
            ).astype(BF16)

    def end_right(self):
        for h in range(2):
            self.own(3 + h).wait()
            self.each_z(lambda t: self.z1c(h, self.z, t).wait_recv())

    def drain(self):
        self.each_z(lambda t: self.z0(t, self.z).wait_send())
        for kind in range(2):
            self.each_w(lambda t: self.wc(kind, t, self.w).wait_send())
        for h in range(2):
            self.each_z(lambda t: self.z1c(h, t, self.z).wait_send())


def kernel(
    nz,
    nw,
    ns,
    q_ref,
    p_ref,
    req_ref,
    cnt_ref,
    neg_ref,
    to_w,
    to_w_t,
    to_z,
    expand,
    column,
    swap,
    spread,
    place,
    dq_ref,
    dp_ref,
    loss_ref,
    ask0,
    ask1,
    ask2,
    ask3,
    qb,
    pb,
    qlen,
    plen,
    ps,
    qs,
    x1,
    y1,
    x2,
    y2,
    bufs1,
    bufs2,
    power,
    wrow,
    wt,
    wt_in,
    hard_w,
    pick,
    pick_t,
    gq,
    gp,
    l1,
    l2,
    l3,
    az_s,
    az_r,
    aw_s,
    aw_r,
    sh_s,
    sh_r,
    zs,
    zr,
    ws,
    wr,
    ls,
    wt_s,
    wt_r,
    lz_s,
    lz_r,
    lw_s,
    lw_r,
    lsub_s,
    lsub_r,
):
    me = lax.axis_index("dp")
    sub = lax.axis_index("sub")
    ndp = nz * nw
    z, w = me // nw, lax.rem(me, nw)
    rows, depth = q_ref.shape
    slots = ndp * CAP
    tiles = depth // TILE
    spot = (nz, nw, z, w, sub)
    ex = [
        Exchange(
            spot,
            (x1, x2)[i],
            (y1, y2)[i],
            (bufs1, bufs2)[i],
            [s.at[i] for s in (zs, zr, ws, wr, ls)],
            to_w,
            to_w_t,
            to_z,
        )
        for i in range(2)
    ]
    along = ex[0]

    def dp_at(k):
        return lax.rem(me + (k + ndp), ndp)

    barrier = pltpu.get_barrier_semaphore()

    def greet(device):
        pl.semaphore_signal(barrier, inc=1, device_id=device, device_id_type=MESH)

    along.each_z(lambda t: greet(along.z_dev(t)))
    along.each_w(lambda t: greet(along.w_dev(t)))
    for k in range(1, SHIFTS):
        greet((dp_at(k), sub))
        greet((dp_at(-k), sub))

    def each_sub(act):
        lax.fori_loop(1, ns, lambda k, n: (act(lax.rem(sub + k, ns)), n)[1], 0)

    each_sub(lambda t: greet((me, t)))

    ask0[...] = jnp.zeros_like(ask0)
    ask0[:, pl.ds(0, CAP)] = req_ref[0].astype(F32)

    def unit(ref, out, length):
        total = jnp.zeros((rows, 1), F32)
        for i in range(tiles):
            v = ref[:, pl.ds(i * TILE, TILE)].astype(F32)
            total = total + jnp.sum(v * v, axis=1, keepdims=True)
        size = jnp.sqrt(total + EPSILON)
        length[...] = size
        for i in range(tiles):
            cols = pl.ds(i * TILE, TILE)
            out[:, cols] = (ref[:, cols].astype(F32) / size).astype(BF16)

    unit(p_ref, pb, plen)
    unit(q_ref, qb, qlen)
    pl.semaphore_wait(barrier, (nz - 1) + (nw - 1) + 2 * (SHIFTS - 1) + (ns - 1))

    def ask_z(to, frm):
        return pltpu.make_async_remote_copy(
            ask0.at[at(to, nw)], ask1.at[at(frm, nw)], az_s.at[to], az_r.at[frm],
            device_id=along.z_dev(to), device_id_type=MESH,
        )

    def ask_w(to, frm):
        return pltpu.make_async_remote_copy(
            ask2.at[at(to, nz)], ask3.at[at(frm, nz)], aw_s.at[to], aw_r.at[frm],
            device_id=along.w_dev(to), device_id_type=MESH,
        )

    def shift(k, side):
        own, held = ((pb, ps), (qb, qs))[side]
        return pltpu.make_async_remote_copy(
            own if k == 0 else held.at[k - 1],
            held.at[k],
            sh_s.at[side, k],
            sh_r.at[side, k],
            device_id=(dp_at(1 - 2 * side), sub),
            device_id_type=MESH,
        )

    along.each_z(lambda t: ask_z(t, z).start())
    for side in range(2):
        shift(0, side).start()
    ask1[at(z, nw), :] = ask0[at(z, nw), :]

    def logits(held):
        def body(i, total):
            cols = at(i, TILE)
            return total + mm_nt(qb[:, cols], held[:, cols])

        return SHARPNESS * lax.fori_loop(0, tiles, body, jnp.zeros((rows, rows), F32))

    along.each_z(lambda t: ask_z(z, t).wait_recv())
    ask2[...] = mm(swap[...], ask1[...].astype(BF16))
    along.each_w(lambda t: ask_w(t, w).start())
    ask3[at(w, nz), :] = ask2[at(w, nz), :]
    first = logits(pb)
    power[0] = jnp.exp(first)
    lane = lax.broadcasted_iota(jnp.int32, (rows, rows), 1)
    row = lax.broadcasted_iota(jnp.int32, (rows, rows), 0)
    eye = jnp.where(lane == row, 1.0, 0.0).astype(F32)
    diagonal = jnp.sum(first * eye, axis=1, keepdims=True)
    along.each_w(lambda t: ask_w(w, t).wait_recv())
    asked = mm(expand[...], ask3[...].astype(BF16))
    asked = jnp.sum(asked * column[...], axis=1, keepdims=True)
    picked = jnp.where(
        asked == lax.broadcasted_iota(jnp.int32, (slots, rows), 1).astype(F32), 1.0, 0.0
    ).astype(F32)
    pick[...] = picked.astype(BF16)
    pick_t[...] = picked.T.astype(BF16)

    half_tiles = tiles // 2

    def gather_rows(i, n):
        cols = at(i, TILE)
        x1[:, cols] = mm(pick[...], pb[:, cols]).astype(BF16)
        return n

    lax.fori_loop(0, half_tiles, gather_rows, 0)
    ex[0].start_left()
    lax.fori_loop(half_tiles, tiles, gather_rows, 0)
    ex[0].start_right()

    slot = lax.broadcasted_iota(jnp.int32, (rows, slots), 1)
    chosen = jnp.zeros((rows, slots), F32)
    for n in range(neg_ref.shape[1]):
        chosen = chosen + jnp.where(neg_ref[:, n : n + 1] == slot, 1.0, 0.0)
    limits = jnp.broadcast_to(cnt_ref[...].astype(F32), (8, ndp)).astype(BF16)
    live = jnp.where(place[...] < mm(limits, spread[...]), 1.0, 0.0)
    gq[:, pl.ds(0, slots)] = chosen * live[0:1]

    for side in range(2):
        shift(0, side).wait_recv()
        shift(1, side).start()
    power[1] = jnp.exp(logits(ps.at[0]))
    ex[0].turn_left()
    for side in range(2):
        shift(1, side).wait_recv()
        shift(2, side).start()
    power[2] = jnp.exp(logits(ps.at[1]))
    ex[0].turn_right()
    for side in range(2):
        shift(2, side).wait_recv()
    power[3] = jnp.exp(logits(ps.at[2]))
    ex[0].end_left()
    ex[0].end_right()

    def hard_logits(i, total):
        cols = at(i, TILE)
        return total + mm_nt(qb[:, cols], y1[:, cols])

    hard = lax.fori_loop(0, tiles, hard_logits, jnp.zeros((rows, slots), F32))
    hard = jnp.exp(SHARPNESS * hard) * gq[:, pl.ds(0, slots)]
    totals = jnp.sum(hard, axis=1, keepdims=True)
    for k in range(SHIFTS):
        totals = totals + jnp.sum(power[k], axis=1, keepdims=True)
    hard = hard / totals
    hard_w[...] = hard.astype(BF16)
    hard_t = hard.T.astype(BF16)

    def slot_sums(i, n):
        cols = at(i, TILE)
        x2[:, cols] = (SHARPNESS * mm(hard_t, qb[:, cols])).astype(BF16)
        return n

    lax.fori_loop(0, half_tiles, slot_sums, 0)
    ex[1].start_left()
    lax.fori_loop(half_tiles, tiles, slot_sums, 0)
    ex[1].start_right()

    def wt_copy(k):
        return pltpu.make_async_remote_copy(
            wt.at[k], wt_in.at[k - 1], wt_s.at[k - 1], wt_r.at[k - 1],
            device_id=(dp_at(-k), sub), device_id_type=MESH,
        )

    for k in range(SHIFTS):
        weight = power[k] / totals
        if k == 0:
            weight = weight - eye
        wrow[k] = weight.astype(BF16)
        wt[k] = weight.T.astype(BF16)
        if k:
            wt_copy(k).start()

    part = jnp.sum(jnp.log(totals) - diagonal)

    def lz(to, frm):
        return pltpu.make_async_remote_copy(
            l1.at[z], l1.at[frm], lz_s.at[to], lz_r.at[frm],
            device_id=along.z_dev(to), device_id_type=MESH,
        )

    def lw(to, frm):
        return pltpu.make_async_remote_copy(
            l2.at[w], l2.at[frm], lw_s.at[to], lw_r.at[frm],
            device_id=along.w_dev(to), device_id_type=MESH,
        )

    def lsub(to, frm):
        return pltpu.make_async_remote_copy(
            l3.at[sub], l3.at[frm], lsub_s.at[to], lsub_r.at[frm],
            device_id=(me, to), device_id_type=MESH,
        )

    def ordered_sum(ref):
        total = ref[0]
        for i in range(1, ref.shape[0]):
            total = total + ref[i]
        return total

    l1[pl.ds(z, 1)] = jnp.broadcast_to(part, (1, 8, 128))
    along.each_z(lambda t: lz(t, z).start())

    def project(raw, length, grad, out):
        size = length[...]

        def radial(i, total):
            cols = at(i, TILE)
            return total + jnp.sum(
                raw[:, cols].astype(F32) / size * grad[:, cols], axis=1, keepdims=True
            )

        along_unit = lax.fori_loop(0, tiles, radial, jnp.zeros((rows, 1), F32))

        def write(i, n):
            cols = at(i, TILE)
            u = raw[:, cols].astype(F32) / size
            out[:, cols] = ((grad[:, cols] - u * along_unit) / size).astype(BF16)
            return n

        lax.fori_loop(0, tiles, write, 0)

    def query_side(i, n):
        cols = at(i, TILE)
        total = mm(hard_w[...], y1[:, cols]) + mm(wrow[0], pb[:, cols])
        for k in range(1, SHIFTS):
            total = total + mm(wrow[k], ps[k - 1, :, cols])
        gq[:, cols] = SHARPNESS * total
        return n

    lax.fori_loop(0, tiles, query_side, 0)

    along.each_z(lambda t: lz(z, t).wait_recv())
    l2[pl.ds(w, 1)] = ordered_sum(l1)[None]
    along.each_w(lambda t: lw(t, w).start())

    project(q_ref, qlen, gq, dq_ref)

    ex[1].turn_left()

    for k in range(1, SHIFTS):
        wt_copy(k).wait_recv()

    def passage_side(i, n):
        cols = at(i, TILE)
        total = mm(wt[0], qb[:, cols])
        for k in range(1, SHIFTS):
            total = total + mm(wt_in[k - 1], qs[k - 1, :, cols])
        gp[:, cols] = SHARPNESS * total
        return n

    lax.fori_loop(0, tiles, passage_side, 0)
    along.each_w(lambda t: lw(w, t).wait_recv())
    l3[pl.ds(sub, 1)] = ordered_sum(l2)[None]
    each_sub(lambda t: lsub(t, sub).start())

    ex[1].turn_right()

    each_sub(lambda t: lsub(sub, t).wait_recv())
    loss_ref[...] = ordered_sum(l3) / float(rows * ndp * ns)

    ex[1].end_left()
    ex[1].end_right()

    def add_returned(i, n):
        cols = at(i, TILE)
        gp[:, cols] = gp[:, cols] + mm(pick_t[...], y2[:, cols])
        return n

    lax.fori_loop(0, tiles, add_returned, 0)
    project(p_ref, plen, gp, dp_ref)

    along.each_z(lambda t: ask_z(t, z).wait_send())
    along.each_w(lambda t: ask_w(t, w).wait_send())
    for k in range(SHIFTS - 1):
        for side in range(2):
            shift(k, side).wait_send()
    for k in range(1, SHIFTS):
        wt_copy(k).wait_send()
    along.each_z(lambda t: lz(t, z).wait_send())
    along.each_w(lambda t: lw(t, w).wait_send())
    each_sub(lambda t: lsub(t, sub).wait_send())
    for e in ex:
        e.drain()


def on_device(nz, nw, ns, queries, passages, requests, counts, neg_slot):
    rows, depth = queries.shape
    ndp = nz * nw
    slots = ndp * CAP
    half, quarter = depth // 2, depth // 4
    dma = pltpu.SemaphoreType.DMA
    v = pltpu.VMEM
    wide = lambda: [
        v((slots, half), BF16),
        v((2 * slots, quarter), BF16),
        v((2 * slots, quarter), BF16),
        v((2 * slots, quarter), BF16),
        v((2 * slots, quarter), BF16),
        v((2 * slots, quarter), BF16),
    ]
    n = SHIFTS - 1
    scratch = (
        [v((ndp, 128), F32)] * 4
        + [v((rows, depth), BF16)] * 2
        + [v((rows, 1), F32)] * 2
        + [v((n, rows, depth), BF16)] * 2
        + [v((slots, depth), BF16)] * 4
        + [wide(), wide()]
        + [v((SHIFTS, rows, rows), F32)]
        + [v((SHIFTS, rows, rows), BF16)] * 2
        + [v((n, rows, rows), BF16)]
        + [v((rows, slots), BF16), v((slots, rows), BF16), v((rows, slots), BF16)]
        + [v((rows, depth), F32)] * 2
        + [v((nz, 8, 128), F32), v((nw, 8, 128), F32), v((ns, 8, 128), F32)]
        + [dma((nz,)), dma((nz,)), dma((nw,)), dma((nw,))]
        + [dma((2, n)), dma((2, n))]
        + [dma((2, 3, nz)), dma((2, 3, nz)), dma((2, 2, nw)), dma((2, 2, nw)), dma((2, 5))]
        + [dma((n,)), dma((n,))]
        + [dma((nz,)), dma((nz,)), dma((nw,)), dma((nw,)), dma((ns,)), dma((ns,))]

    )
    vmem = pl.BlockSpec(memory_space=pltpu.VMEM)
    fixed = tables(nz, nw)
    flops = 2 * rows * depth * (SHIFTS * rows * 3 + slots * 5) + 14 * slots * slots * depth
    dq, dp, loss = pl.pallas_call(
        functools.partial(kernel, nz, nw, ns),
        out_shape=(
            jax.ShapeDtypeStruct((rows, depth), BF16),
            jax.ShapeDtypeStruct((rows, depth), BF16),
            jax.ShapeDtypeStruct((8, 128), F32),
        ),
        in_specs=[vmem] * (5 + len(fixed)),
        out_specs=(vmem, vmem, vmem),
        scratch_shapes=scratch,
        compiler_params=pltpu.CompilerParams(
            collective_id=0, has_side_effects=True, vmem_limit_bytes=60 << 20
        ),
        cost_estimate=pl.CostEstimate(
            flops=flops, bytes_accessed=12 * rows * depth, transcendentals=rows * slots * 2
        ),
    )(queries, passages, requests, counts, neg_slot, *fixed)
    return dq, dp, loss[0, 0]


def solution(mesh):
    ndp, ns = mesh.shape["dp"], mesh.shape["sub"]
    nz = Z_SIZE
    placed = (
        P(("dp", "sub"), None),
        P(("dp", "sub"), None),
        P(("dp", "sub"), None, None),
        P(("dp", "sub"), None),
        P(("dp", "sub"), None),
    )
    return jax.shard_map(
        functools.partial(on_device, nz, ndp // nz, ns),
        mesh=mesh,
        in_specs=placed,
        out_specs=(P(("dp", "sub"), None), P(("dp", "sub"), None), P()),
        check_vma=False,
    )
```

```python
import functools

import jax
import jax.numpy as jnp
import numpy as np
from jax import lax
from jax.experimental import pallas as pl
from jax.experimental.pallas import tpu as pltpu
from jax.sharding import PartitionSpec as P

SHIFTS = 4
CAP = 3
SHARPNESS = 50.0
EPSILON = 1e-06
Z_SIZE = 8
TILE = 256
WIDE = 512
MESH = pl.DeviceIdType.MESH
F32 = jnp.float32
BF16 = jnp.bfloat16


def tables(nz, nw):
    slots = nz * nw * CAP
    z, w, c = np.meshgrid(np.arange(nz), np.arange(nw), np.arange(CAP), indexing="ij")
    slot = ((z * nw + w) * CAP + c).reshape(-1)
    to_w = np.zeros((2 * slots, 2 * slots), np.float32)
    to_z = np.zeros((2 * slots, 2 * slots), np.float32)
    for half in range(2):
        by_w = (((w * 2 + half) * nz + z) * CAP + c).reshape(-1)
        by_z = (((z * 2 + half) * nw + w) * CAP + c).reshape(-1)
        to_w[by_w, half * slots + slot] = 1
        to_z[by_z, by_w] = 1
    expand = np.zeros((slots, nz * nw), np.float32)
    expand[slot, (w * nz + z).reshape(-1)] = 1
    column = np.zeros((slots, 128), np.float32)
    column[slot, c.reshape(-1)] = 1
    swap = np.zeros((nz * nw, nz * nw), np.float32)
    zz, ww = np.meshgrid(np.arange(nz), np.arange(nw), indexing="ij")
    swap[(ww * nz + zz).reshape(-1), (zz * nw + ww).reshape(-1)] = 1
    spread = np.zeros((nz * nw, slots), np.float32)
    spread[slot // CAP, slot] = 1
    place = np.broadcast_to((np.arange(slots) % CAP).astype(np.float32), (8, slots))
    b = lambda v: jnp.asarray(np.ascontiguousarray(v), BF16)
    return (
        b(to_w),
        b(to_w.T),
        b(to_z),
        b(expand),
        jnp.asarray(column),
        b(swap),
        b(spread),
        jnp.asarray(np.ascontiguousarray(place)),
    )


def mm(a, b):
    return jnp.dot(a, b, preferred_element_type=F32)


def mm_nt(a, b):
    return lax.dot_general(a, b, (((1,), (1,)), ((), ())), preferred_element_type=F32)


def at(index, size):
    return pl.ds(pl.multiple_of(index * size, size), size)


class Exchange:
    def __init__(self, place, x, y, bufs, sems, to_w, to_w_t, to_z):
        self.nz, self.nw, self.z, self.w, self.sub = place
        self.x, self.y = x, y
        self.r0, self.w0, self.rw0, self.w1, self.r1, self.z1 = bufs
        self.zs, self.zr, self.ws, self.wr, self.ls = sems
        self.to_w, self.to_w_t, self.to_z = to_w, to_w_t, to_z
        self.half = x.shape[1] // 2
        self.quarter = self.half // 2
        self.slots = x.shape[0]
        self.zrows = self.nw * CAP
        self.wrows = 2 * self.nz * CAP

    def z_peer(self, k):
        return lax.rem(self.z + k, self.nz)

    def w_peer(self, k):
        return lax.rem(self.w + k, self.nw)

    def z_dev(self, t):
        return (t * self.nw + self.w, self.sub)

    def w_dev(self, t):
        return (self.z * self.nw + t, self.sub)

    def z0(self, to, frm):
        return pltpu.make_async_remote_copy(
            self.x.at[at(to, self.zrows), pl.ds(0, self.half)],
            self.r0.at[at(frm, self.zrows)],
            self.zs.at[0, to],
            self.zr.at[0, frm],
            device_id=self.z_dev(to),
            device_id_type=MESH,
        )

    def z1c(self, h, to, frm):
        rows = pl.ds(pl.multiple_of(to * 2 * self.zrows + h * self.zrows, self.zrows), self.zrows)
        return pltpu.make_async_remote_copy(
            self.z1.at[rows],
            self.y.at[at(frm, self.zrows), pl.ds(self.half + h * self.quarter, self.quarter)],
            self.zs.at[1 + h, to],
            self.zr.at[1 + h, frm],
            device_id=self.z_dev(to),
            device_id_type=MESH,
        )

    def wc(self, kind, to, frm):
        src, dst = ((self.w0, self.rw0), (self.w1, self.r1))[kind]
        return pltpu.make_async_remote_copy(
            src.at[at(to, self.wrows)],
            dst.at[at(frm, self.wrows)],
            self.ws.at[kind, to],
            self.wr.at[kind, frm],
            device_id=self.w_dev(to),
            device_id_type=MESH,
        )

    def own(self, which):
        if which == 0:
            return pltpu.make_async_copy(
                self.x.at[at(self.z, self.zrows), pl.ds(0, self.half)],
                self.r0.at[at(self.z, self.zrows)],
                self.ls.at[0],
            )
        if which in (1, 2):
            src, dst = ((self.w0, self.rw0), (self.w1, self.r1))[which - 1]
            return pltpu.make_async_copy(
                src.at[at(self.w, self.wrows)], dst.at[at(self.w, self.wrows)], self.ls.at[which]
            )
        h = which - 3
        rows = pl.ds(
            pl.multiple_of(self.z * 2 * self.zrows + h * self.zrows, self.zrows), self.zrows
        )
        return pltpu.make_async_copy(
            self.z1.at[rows],
            self.y.at[at(self.z, self.zrows), pl.ds(self.half + h * self.quarter, self.quarter)],
            self.ls.at[which],
        )

    def each_z(self, act):
        lax.fori_loop(1, self.nz, lambda k, n: (act(self.z_peer(k)), n)[1], 0)

    def each_w(self, act):
        lax.fori_loop(1, self.nw, lambda k, n: (act(self.w_peer(k)), n)[1], 0)

    def reorder_to_w(self, dst, src, first):
        step = self.slots
        left = src[:, pl.ds(first, self.quarter)]
        right = src[:, pl.ds(first + self.quarter, self.quarter)]

        def body(i, n):
            m = self.to_w.at[at(i, step)]
            dst[at(i, step), :] = (
                mm(m[:, pl.ds(0, self.slots)], left)
                + mm(m[:, pl.ds(self.slots, self.slots)], right)
            ).astype(BF16)
            return n

        lax.fori_loop(0, 2 * self.slots // step, body, 0)

    def start_left(self):
        self.each_z(lambda t: self.z0(t, self.z).start())
        self.own(0).start()

    def start_right(self):
        self.reorder_to_w(self.w1, self.x, self.half)
        self.each_w(lambda t: self.wc(1, t, self.w).start())
        self.own(2).start()

    def turn_left(self):
        self.own(0).wait()
        self.each_z(lambda t: self.z0(self.z, t).wait_recv())
        self.reorder_to_w(self.w0, self.r0, 0)
        self.each_w(lambda t: self.wc(0, t, self.w).start())
        self.own(1).start()

    def turn_right(self):
        self.own(2).wait()
        self.each_w(lambda t: self.wc(1, self.w, t).wait_recv())
        step = self.slots

        def body(i, n):
            self.z1[at(i, step), :] = mm(self.to_z[at(i, step), :], self.r1[...]).astype(BF16)
            return n

        lax.fori_loop(0, 2 * self.slots // step, body, 0)
        for h in range(2):
            self.each_z(lambda t: self.z1c(h, t, self.z).start())
            self.own(3 + h).start()

    def end_left(self):
        self.own(1).wait()
        self.each_w(lambda t: self.wc(0, self.w, t).wait_recv())
        for h in range(2):
            self.y[:, pl.ds(h * self.quarter, self.quarter)] = mm(
                self.to_w_t[pl.ds(h * self.slots, self.slots), :], self.rw0[...]
            ).astype(BF16)

    def end_right(self):
        for h in range(2):
            self.own(3 + h).wait()
            self.each_z(lambda t: self.z1c(h, self.z, t).wait_recv())

    def drain(self):
        self.each_z(lambda t: self.z0(t, self.z).wait_send())
        for kind in range(2):
            self.each_w(lambda t: self.wc(kind, t, self.w).wait_send())
        for h in range(2):
            self.each_z(lambda t: self.z1c(h, t, self.z).wait_send())


def kernel(
    nz,
    nw,
    ns,
    q_ref,
    p_ref,
    req_ref,
    cnt_ref,
    neg_ref,
    to_w,
    to_w_t,
    to_z,
    expand,
    column,
    swap,
    spread,
    place,
    dq_ref,
    dp_ref,
    loss_ref,
    ask0,
    ask1,
    ask2,
    ask3,
    qb,
    pb,
    qlen,
    plen,
    ps,
    qs,
    x1,
    y1,
    x2,
    y2,
    bufs1,
    bufs2,
    power,
    wrow,
    wt,
    wt_in,
    hard_w,
    pick,
    pick_t,
    gq,
    gp,
    l1,
    l2,
    l3,
    az_s,
    az_r,
    aw_s,
    aw_r,
    sh_s,
    sh_r,
    zs,
    zr,
    ws,
    wr,
    ls,
    wt_s,
    wt_r,
    lz_s,
    lz_r,
    lw_s,
    lw_r,
    lsub_s,
    lsub_r,
):
    me = lax.axis_index("dp")
    sub = lax.axis_index("sub")
    ndp = nz * nw
    z, w = me // nw, lax.rem(me, nw)
    rows, depth = q_ref.shape
    slots = ndp * CAP
    tiles = depth // TILE
    wides = depth // WIDE
    spot = (nz, nw, z, w, sub)
    ex = [
        Exchange(
            spot,
            (x1, x2)[i],
            (y1, y2)[i],
            (bufs1, bufs2)[i],
            [s.at[i] for s in (zs, zr, ws, wr, ls)],
            to_w,
            to_w_t,
            to_z,
        )
        for i in range(2)
    ]
    along = ex[0]

    def dp_at(k):
        return lax.rem(me + (k + ndp), ndp)

    barrier = pltpu.get_barrier_semaphore()

    def greet(device):
        pl.semaphore_signal(barrier, inc=1, device_id=device, device_id_type=MESH)

    along.each_z(lambda t: greet(along.z_dev(t)))
    along.each_w(lambda t: greet(along.w_dev(t)))
    for k in range(1, SHIFTS):
        greet((dp_at(k), sub))
        greet((dp_at(-k), sub))

    def each_sub(act):
        lax.fori_loop(1, ns, lambda k, n: (act(lax.rem(sub + k, ns)), n)[1], 0)

    each_sub(lambda t: greet((me, t)))

    ask0[...] = jnp.zeros_like(ask0)
    ask0[:, pl.ds(0, CAP)] = req_ref[0].astype(F32)

    def unit(ref, out, length):
        total = jnp.zeros((rows, 1), F32)
        for i in range(tiles):
            v = ref[:, pl.ds(i * TILE, TILE)].astype(F32)
            total = total + jnp.sum(v * v, axis=1, keepdims=True)
        size = jnp.sqrt(total + EPSILON)
        length[...] = size
        for i in range(tiles):
            cols = pl.ds(i * TILE, TILE)
            out[:, cols] = (ref[:, cols].astype(F32) / size).astype(BF16)

    unit(p_ref, pb, plen)
    pl.semaphore_wait(barrier, (nz - 1) + (nw - 1) + 2 * (SHIFTS - 1) + (ns - 1))

    def ask_z(to, frm):
        return pltpu.make_async_remote_copy(
            ask0.at[at(to, nw)], ask1.at[at(frm, nw)], az_s.at[to], az_r.at[frm],
            device_id=along.z_dev(to), device_id_type=MESH,
        )

    def ask_w(to, frm):
        return pltpu.make_async_remote_copy(
            ask2.at[at(to, nz)], ask3.at[at(frm, nz)], aw_s.at[to], aw_r.at[frm],
            device_id=along.w_dev(to), device_id_type=MESH,
        )

    def shift(k, side):
        own, held = ((pb, ps), (qb, qs))[side]
        return pltpu.make_async_remote_copy(
            own if k == 0 else held.at[k - 1],
            held.at[k],
            sh_s.at[side, k],
            sh_r.at[side, k],
            device_id=(dp_at(1 - 2 * side), sub),
            device_id_type=MESH,
        )

    along.each_z(lambda t: ask_z(t, z).start())
    shift(0, 0).start()
    unit(q_ref, qb, qlen)
    shift(0, 1).start()
    ask1[at(z, nw), :] = ask0[at(z, nw), :]

    def logits(held):
        def body(i, total):
            cols = at(i, WIDE)
            return total + mm_nt(qb[:, cols], held[:, cols])

        return SHARPNESS * lax.fori_loop(0, wides, body, jnp.zeros((rows, rows), F32), unroll=True)

    along.each_z(lambda t: ask_z(z, t).wait_recv())
    ask2[...] = mm(swap[...], ask1[...].astype(BF16))
    along.each_w(lambda t: ask_w(t, w).start())
    ask3[at(w, nz), :] = ask2[at(w, nz), :]
    first = logits(pb)
    power[0] = jnp.exp(first)
    lane = lax.broadcasted_iota(jnp.int32, (rows, rows), 1)
    row = lax.broadcasted_iota(jnp.int32, (rows, rows), 0)
    eye = jnp.where(lane == row, 1.0, 0.0).astype(F32)
    diagonal = jnp.sum(first * eye, axis=1, keepdims=True)
    along.each_w(lambda t: ask_w(w, t).wait_recv())
    asked = mm(expand[...], ask3[...].astype(BF16))
    asked = jnp.sum(asked * column[...], axis=1, keepdims=True)
    picked = jnp.where(
        asked == lax.broadcasted_iota(jnp.int32, (slots, rows), 1).astype(F32), 1.0, 0.0
    ).astype(F32)
    pick[...] = picked.astype(BF16)
    pick_t[...] = picked.T.astype(BF16)

    half_tiles = tiles // 2

    def gather_rows(i, n):
        cols = at(i, TILE)
        x1[:, cols] = mm(pick[...], pb[:, cols]).astype(BF16)
        return n

    lax.fori_loop(0, half_tiles, gather_rows, 0)
    ex[0].start_left()
    lax.fori_loop(half_tiles, tiles, gather_rows, 0)
    ex[0].start_right()

    slot = lax.broadcasted_iota(jnp.int32, (rows, slots), 1)
    chosen = jnp.zeros((rows, slots), F32)
    for n in range(neg_ref.shape[1]):
        chosen = chosen + jnp.where(neg_ref[:, n : n + 1] == slot, 1.0, 0.0)
    limits = jnp.broadcast_to(cnt_ref[...].astype(F32), (8, ndp)).astype(BF16)
    live = jnp.where(place[...] < mm(limits, spread[...]), 1.0, 0.0)
    gq[:, pl.ds(0, slots)] = chosen * live[0:1]

    for side in range(2):
        shift(0, side).wait_recv()
        shift(1, side).start()
    power[1] = jnp.exp(logits(ps.at[0]))
    ex[0].turn_left()
    for side in range(2):
        shift(1, side).wait_recv()
        shift(2, side).start()
    power[2] = jnp.exp(logits(ps.at[1]))
    ex[0].turn_right()
    ex[0].end_left()
    ex[0].end_right()

    def hard_logits(i, total):
        cols = at(i, WIDE)
        return total + mm_nt(qb[:, cols], y1[:, cols])

    hard = lax.fori_loop(0, wides, hard_logits, jnp.zeros((rows, slots), F32), unroll=True)
    hard = jnp.exp(SHARPNESS * hard) * gq[:, pl.ds(0, slots)]
    shift(2, 0).wait_recv()
    power[3] = jnp.exp(logits(ps.at[2]))
    totals = jnp.sum(hard, axis=1, keepdims=True)
    for k in range(SHIFTS):
        totals = totals + jnp.sum(power[k], axis=1, keepdims=True)
    hard = hard / totals
    hard_w[...] = hard.astype(BF16)
    hard_t = hard.T.astype(BF16)

    def slot_sums(i, n):
        cols = at(i, TILE)
        x2[:, cols] = (SHARPNESS * mm(hard_t, qb[:, cols])).astype(BF16)
        return n

    lax.fori_loop(0, half_tiles, slot_sums, 0, unroll=True)
    ex[1].start_left()
    lax.fori_loop(half_tiles, tiles, slot_sums, 0, unroll=True)
    ex[1].start_right()

    def wt_copy(k):
        return pltpu.make_async_remote_copy(
            wt.at[k], wt_in.at[k - 1], wt_s.at[k - 1], wt_r.at[k - 1],
            device_id=(dp_at(-k), sub), device_id_type=MESH,
        )

    for k in range(SHIFTS):
        weight = power[k] / totals
        if k == 0:
            weight = weight - eye
        wrow[k] = weight.astype(BF16)
        wt[k] = weight.T.astype(BF16)
        if k:
            wt_copy(k).start()

    part = jnp.sum(jnp.log(totals) - diagonal)

    def lz(to, frm):
        return pltpu.make_async_remote_copy(
            l1.at[z], l1.at[frm], lz_s.at[to], lz_r.at[frm],
            device_id=along.z_dev(to), device_id_type=MESH,
        )

    def lw(to, frm):
        return pltpu.make_async_remote_copy(
            l2.at[w], l2.at[frm], lw_s.at[to], lw_r.at[frm],
            device_id=along.w_dev(to), device_id_type=MESH,
        )

    def lsub(to, frm):
        return pltpu.make_async_remote_copy(
            l3.at[sub], l3.at[frm], lsub_s.at[to], lsub_r.at[frm],
            device_id=(me, to), device_id_type=MESH,
        )

    def ordered_sum(ref):
        total = ref[0]
        for i in range(1, ref.shape[0]):
            total = total + ref[i]
        return total

    l1[pl.ds(z, 1)] = jnp.broadcast_to(part, (1, 8, 128))
    along.each_z(lambda t: lz(t, z).start())

    def project(raw, length, grad, out):
        size = length[...]

        def radial(i, total):
            cols = at(i, WIDE)
            return total + jnp.sum(
                raw[:, cols].astype(F32) / size * grad[:, cols], axis=1, keepdims=True
            )

        along_unit = lax.fori_loop(0, wides, radial, jnp.zeros((rows, 1), F32), unroll=True)

        def write(i, n):
            cols = at(i, WIDE)
            u = raw[:, cols].astype(F32) / size
            out[:, cols] = ((grad[:, cols] - u * along_unit) / size).astype(BF16)
            return n

        lax.fori_loop(0, wides, write, 0)

    def query_side(i, n):
        cols = at(i, WIDE)
        total = mm(hard_w[...], y1[:, cols]) + mm(wrow[0], pb[:, cols])
        for k in range(1, SHIFTS):
            total = total + mm(wrow[k], ps[k - 1, :, cols])
        gq[:, cols] = SHARPNESS * total
        return n

    lax.fori_loop(0, wides, query_side, 0)

    along.each_z(lambda t: lz(z, t).wait_recv())
    l2[pl.ds(w, 1)] = ordered_sum(l1)[None]
    along.each_w(lambda t: lw(t, w).start())

    project(q_ref, qlen, gq, dq_ref)

    for k in range(1, SHIFTS):
        wt_copy(k).wait_recv()
    shift(2, 1).wait_recv()

    def passage_side(i, n):
        cols = at(i, WIDE)
        total = mm(wt[0], qb[:, cols])
        for k in range(1, SHIFTS):
            total = total + mm(wt_in[k - 1], qs[k - 1, :, cols])
        gp[:, cols] = SHARPNESS * total
        return n

    lax.fori_loop(0, wides, passage_side, 0)
    ex[1].turn_left()
    ex[1].turn_right()

    along.each_w(lambda t: lw(w, t).wait_recv())
    l3[pl.ds(sub, 1)] = ordered_sum(l2)[None]
    each_sub(lambda t: lsub(t, sub).start())


    each_sub(lambda t: lsub(sub, t).wait_recv())
    loss_ref[...] = (ordered_sum(l3) / float(rows * ndp * ns))[0:1, 0:1]

    def add_returned(i, n):
        cols = at(i, TILE)
        gp[:, cols] = gp[:, cols] + mm(pick_t[...], y2[:, cols])
        return n

    ex[1].end_left()
    lax.fori_loop(0, half_tiles, add_returned, 0, unroll=True)
    ex[1].end_right()
    lax.fori_loop(half_tiles, tiles, add_returned, 0, unroll=True)
    project(p_ref, plen, gp, dp_ref)

    along.each_z(lambda t: ask_z(t, z).wait_send())
    along.each_w(lambda t: ask_w(t, w).wait_send())
    for k in range(SHIFTS - 1):
        for side in range(2):
            shift(k, side).wait_send()
    for k in range(1, SHIFTS):
        wt_copy(k).wait_send()
    along.each_z(lambda t: lz(t, z).wait_send())
    along.each_w(lambda t: lw(t, w).wait_send())
    each_sub(lambda t: lsub(t, sub).wait_send())
    for e in ex:
        e.drain()


def on_device(nz, nw, ns, queries, passages, requests, counts, neg_slot):
    rows, depth = queries.shape
    ndp = nz * nw
    slots = ndp * CAP
    half, quarter = depth // 2, depth // 4
    dma = pltpu.SemaphoreType.DMA
    v = pltpu.VMEM
    wide = lambda: [
        v((slots, half), BF16),
        v((2 * slots, quarter), BF16),
        v((2 * slots, quarter), BF16),
        v((2 * slots, quarter), BF16),
        v((2 * slots, quarter), BF16),
        v((2 * slots, quarter), BF16),
    ]
    n = SHIFTS - 1
    scratch = (
        [v((ndp, 128), F32)] * 4
        + [v((rows, depth), BF16)] * 2
        + [v((rows, 1), F32)] * 2
        + [v((n, rows, depth), BF16)] * 2
        + [v((slots, depth), BF16)] * 4
        + [wide(), wide()]
        + [v((SHIFTS, rows, rows), F32)]
        + [v((SHIFTS, rows, rows), BF16)] * 2
        + [v((n, rows, rows), BF16)]
        + [v((rows, slots), BF16), v((slots, rows), BF16), v((rows, slots), BF16)]
        + [v((rows, depth), F32)] * 2
        + [v((nz, 8, 128), F32), v((nw, 8, 128), F32), v((ns, 8, 128), F32)]
        + [dma((nz,)), dma((nz,)), dma((nw,)), dma((nw,))]
        + [dma((2, n)), dma((2, n))]
        + [dma((2, 3, nz)), dma((2, 3, nz)), dma((2, 2, nw)), dma((2, 2, nw)), dma((2, 5))]
        + [dma((n,)), dma((n,))]
        + [dma((nz,)), dma((nz,)), dma((nw,)), dma((nw,)), dma((ns,)), dma((ns,))]

    )
    vmem = pl.BlockSpec(memory_space=pltpu.VMEM)
    fixed = tables(nz, nw)
    flops = 2 * rows * depth * (SHIFTS * rows * 3 + slots * 5) + 14 * slots * slots * depth
    dq, dp, loss = pl.pallas_call(
        functools.partial(kernel, nz, nw, ns),
        out_shape=(
            jax.ShapeDtypeStruct((rows, depth), BF16),
            jax.ShapeDtypeStruct((rows, depth), BF16),
            jax.ShapeDtypeStruct((1, 1), F32),
        ),
        in_specs=[vmem] * (5 + len(fixed)),
        out_specs=(vmem, vmem, vmem),
        scratch_shapes=scratch,
        compiler_params=pltpu.CompilerParams(
            collective_id=0, has_side_effects=True, vmem_limit_bytes=60 << 20
        ),
        cost_estimate=pl.CostEstimate(
            flops=flops, bytes_accessed=12 * rows * depth, transcendentals=rows * slots * 2
        ),
    )(queries, passages, requests, counts, neg_slot, *fixed)
    return dq, dp, loss.reshape(())


def solution(mesh):
    ndp, ns = mesh.shape["dp"], mesh.shape["sub"]
    nz = Z_SIZE
    placed = (
        P(("dp", "sub"), None),
        P(("dp", "sub"), None),
        P(("dp", "sub"), None, None),
        P(("dp", "sub"), None),
        P(("dp", "sub"), None),
    )
    return jax.shard_map(
        functools.partial(on_device, nz, ndp // nz, ns),
        mesh=mesh,
        in_specs=placed,
        out_specs=(P(("dp", "sub"), None), P(("dp", "sub"), None), P()),
        check_vma=False,
    )
```

```python
import functools

import jax
import jax.numpy as jnp
import numpy as np
from jax import lax
from jax.experimental import pallas as pl
from jax.experimental.pallas import tpu as pltpu
from jax.sharding import PartitionSpec as P

SHIFTS = 4
CAP = 3
SHARPNESS = 50.0
EPSILON = 1e-06
Z_SIZE = 8
TILE = 256
WIDE = 512
MESH = pl.DeviceIdType.MESH
F32 = jnp.float32
BF16 = jnp.bfloat16


def tables(nz, nw):
    slots = nz * nw * CAP
    z, w, c = np.meshgrid(np.arange(nz), np.arange(nw), np.arange(CAP), indexing="ij")
    slot = ((z * nw + w) * CAP + c).reshape(-1)
    to_w = np.zeros((2 * slots, 2 * slots), np.float32)
    to_z = np.zeros((2 * slots, 2 * slots), np.float32)
    for half in range(2):
        by_w = (((w * 2 + half) * nz + z) * CAP + c).reshape(-1)
        by_z = (((z * 2 + half) * nw + w) * CAP + c).reshape(-1)
        to_w[by_w, half * slots + slot] = 1
        to_z[by_z, by_w] = 1
    expand = np.zeros((slots, nz * nw), np.float32)
    expand[slot, (w * nz + z).reshape(-1)] = 1
    column = np.zeros((slots, 128), np.float32)
    column[slot, c.reshape(-1)] = 1
    swap = np.zeros((nz * nw, nz * nw), np.float32)
    zz, ww = np.meshgrid(np.arange(nz), np.arange(nw), indexing="ij")
    swap[(ww * nz + zz).reshape(-1), (zz * nw + ww).reshape(-1)] = 1
    spread = np.zeros((nz * nw, slots), np.float32)
    spread[slot // CAP, slot] = 1
    place = np.broadcast_to((np.arange(slots) % CAP).astype(np.float32), (8, slots))
    b = lambda v: jnp.asarray(np.ascontiguousarray(v), BF16)
    return (
        b(to_w),
        b(to_w.T),
        b(to_z),
        b(expand),
        jnp.asarray(column),
        b(swap),
        b(spread),
        jnp.asarray(np.ascontiguousarray(place)),
    )


def mm(a, b):
    return jnp.dot(a, b, preferred_element_type=F32)


def mm_nt(a, b):
    return lax.dot_general(a, b, (((1,), (1,)), ((), ())), preferred_element_type=F32)


def at(index, size):
    return pl.ds(pl.multiple_of(index * size, size), size)


class Exchange:
    def __init__(self, place, x, y, bufs, sems, to_w, to_w_t, to_z):
        self.nz, self.nw, self.z, self.w, self.sub = place
        self.x, self.y = x, y
        self.r0, self.w0, self.rw0, self.w1, self.r1, self.z1 = bufs
        self.zs, self.zr, self.ws, self.wr, self.ls = sems
        self.to_w, self.to_w_t, self.to_z = to_w, to_w_t, to_z
        self.half = x.shape[1] // 2
        self.quarter = self.half // 2
        self.slots = x.shape[0]
        self.zrows = self.nw * CAP
        self.wrows = 2 * self.nz * CAP

    def z_peer(self, k):
        return lax.rem(self.z + k, self.nz)

    def w_peer(self, k):
        return lax.rem(self.w + k, self.nw)

    def z_dev(self, t):
        return (t * self.nw + self.w, self.sub)

    def w_dev(self, t):
        return (self.z * self.nw + t, self.sub)

    def z0(self, to, frm):
        return pltpu.make_async_remote_copy(
            self.x.at[at(to, self.zrows), pl.ds(0, self.half)],
            self.r0.at[at(frm, self.zrows)],
            self.zs.at[0, to],
            self.zr.at[0, frm],
            device_id=self.z_dev(to),
            device_id_type=MESH,
        )

    def z1c(self, h, to, frm):
        rows = pl.ds(pl.multiple_of(to * 2 * self.zrows + h * self.zrows, self.zrows), self.zrows)
        return pltpu.make_async_remote_copy(
            self.z1.at[rows],
            self.y.at[at(frm, self.zrows), pl.ds(self.half + h * self.quarter, self.quarter)],
            self.zs.at[1 + h, to],
            self.zr.at[1 + h, frm],
            device_id=self.z_dev(to),
            device_id_type=MESH,
        )

    def wc(self, kind, to, frm):
        src, dst = ((self.w0, self.rw0), (self.w1, self.r1))[kind]
        return pltpu.make_async_remote_copy(
            src.at[at(to, self.wrows)],
            dst.at[at(frm, self.wrows)],
            self.ws.at[kind, to],
            self.wr.at[kind, frm],
            device_id=self.w_dev(to),
            device_id_type=MESH,
        )

    def own(self, which):
        if which == 0:
            return pltpu.make_async_copy(
                self.x.at[at(self.z, self.zrows), pl.ds(0, self.half)],
                self.r0.at[at(self.z, self.zrows)],
                self.ls.at[0],
            )
        if which in (1, 2):
            src, dst = ((self.w0, self.rw0), (self.w1, self.r1))[which - 1]
            return pltpu.make_async_copy(
                src.at[at(self.w, self.wrows)], dst.at[at(self.w, self.wrows)], self.ls.at[which]
            )
        h = which - 3
        rows = pl.ds(
            pl.multiple_of(self.z * 2 * self.zrows + h * self.zrows, self.zrows), self.zrows
        )
        return pltpu.make_async_copy(
            self.z1.at[rows],
            self.y.at[at(self.z, self.zrows), pl.ds(self.half + h * self.quarter, self.quarter)],
            self.ls.at[which],
        )

    def each_z(self, act):
        lax.fori_loop(1, self.nz, lambda k, n: (act(self.z_peer(k)), n)[1], 0)

    def each_w(self, act):
        lax.fori_loop(1, self.nw, lambda k, n: (act(self.w_peer(k)), n)[1], 0)

    def reorder_to_w(self, dst, src, first):
        step = self.slots
        left = src[:, pl.ds(first, self.quarter)]
        right = src[:, pl.ds(first + self.quarter, self.quarter)]

        def body(i, n):
            m = self.to_w.at[at(i, step)]
            dst[at(i, step), :] = (
                mm(m[:, pl.ds(0, self.slots)], left)
                + mm(m[:, pl.ds(self.slots, self.slots)], right)
            ).astype(BF16)
            return n

        lax.fori_loop(0, 2 * self.slots // step, body, 0)

    def start_left(self):
        self.each_z(lambda t: self.z0(t, self.z).start())
        self.own(0).start()

    def start_right(self):
        self.reorder_to_w(self.w1, self.x, self.half)
        self.each_w(lambda t: self.wc(1, t, self.w).start())
        self.own(2).start()

    def turn_left(self):
        self.own(0).wait()
        self.each_z(lambda t: self.z0(self.z, t).wait_recv())
        self.reorder_to_w(self.w0, self.r0, 0)
        self.each_w(lambda t: self.wc(0, t, self.w).start())
        self.own(1).start()

    def turn_right(self):
        self.own(2).wait()
        self.each_w(lambda t: self.wc(1, self.w, t).wait_recv())
        step = self.slots

        def body(i, n):
            self.z1[at(i, step), :] = mm(self.to_z[at(i, step), :], self.r1[...]).astype(BF16)
            return n

        lax.fori_loop(0, 2 * self.slots // step, body, 0)
        for h in range(2):
            self.each_z(lambda t: self.z1c(h, t, self.z).start())
            self.own(3 + h).start()

    def end_left(self):
        self.own(1).wait()
        self.each_w(lambda t: self.wc(0, self.w, t).wait_recv())
        for h in range(2):
            self.y[:, pl.ds(h * self.quarter, self.quarter)] = mm(
                self.to_w_t[pl.ds(h * self.slots, self.slots), :], self.rw0[...]
            ).astype(BF16)

    def end_right(self):
        for h in range(2):
            self.own(3 + h).wait()
            self.each_z(lambda t: self.z1c(h, self.z, t).wait_recv())

    def drain(self):
        self.each_z(lambda t: self.z0(t, self.z).wait_send())
        for kind in range(2):
            self.each_w(lambda t: self.wc(kind, t, self.w).wait_send())
        for h in range(2):
            self.each_z(lambda t: self.z1c(h, t, self.z).wait_send())


def kernel(
    nz,
    nw,
    ns,
    q_ref,
    p_ref,
    req_ref,
    cnt_ref,
    neg_ref,
    to_w,
    to_w_t,
    to_z,
    expand,
    column,
    swap,
    spread,
    place,
    dq_ref,
    dp_ref,
    loss_ref,
    ask0,
    ask1,
    ask2,
    ask3,
    qb,
    pb,
    qlen,
    plen,
    ps,
    qs,
    x1,
    y1,
    x2,
    y2,
    bufs1,
    bufs2,
    power,
    wrow,
    wt,
    wt_in,
    hard_w,
    pick,
    pick_t,
    gq,
    gp,
    l1,
    l2,
    l3,
    az_s,
    az_r,
    aw_s,
    aw_r,
    sh_s,
    sh_r,
    zs,
    zr,
    ws,
    wr,
    ls,
    wt_s,
    wt_r,
    lz_s,
    lz_r,
    lw_s,
    lw_r,
    lsub_s,
    lsub_r,
):
    me = lax.axis_index("dp")
    sub = lax.axis_index("sub")
    ndp = nz * nw
    z, w = me // nw, lax.rem(me, nw)
    rows, depth = q_ref.shape
    slots = ndp * CAP
    tiles = depth // TILE
    wides = depth // WIDE
    spot = (nz, nw, z, w, sub)
    ex = [
        Exchange(
            spot,
            (x1, x2)[i],
            (y1, y2)[i],
            (bufs1, bufs2)[i],
            [s.at[i] for s in (zs, zr, ws, wr, ls)],
            to_w,
            to_w_t,
            to_z,
        )
        for i in range(2)
    ]
    along = ex[0]

    def dp_at(k):
        return lax.rem(me + (k + ndp), ndp)

    barrier = pltpu.get_barrier_semaphore()

    def greet(device):
        pl.semaphore_signal(barrier, inc=1, device_id=device, device_id_type=MESH)

    along.each_z(lambda t: greet(along.z_dev(t)))
    along.each_w(lambda t: greet(along.w_dev(t)))
    for k in range(1, SHIFTS):
        greet((dp_at(k), sub))
        greet((dp_at(-k), sub))

    def each_sub(act):
        lax.fori_loop(1, ns, lambda k, n: (act(lax.rem(sub + k, ns)), n)[1], 0)

    each_sub(lambda t: greet((me, t)))

    ask0[...] = jnp.zeros_like(ask0)
    ask0[:, pl.ds(0, CAP)] = req_ref[0].astype(F32)

    def unit(ref, out, length):
        total = jnp.zeros((rows, 1), F32)
        for i in range(tiles):
            v = ref[:, pl.ds(i * TILE, TILE)].astype(F32)
            total = total + jnp.sum(v * v, axis=1, keepdims=True)
        size = jnp.sqrt(total + EPSILON)
        length[...] = size
        for i in range(tiles):
            cols = pl.ds(i * TILE, TILE)
            out[:, cols] = (ref[:, cols].astype(F32) / size).astype(BF16)

    unit(p_ref, pb, plen)
    pl.semaphore_wait(barrier, (nz - 1) + (nw - 1) + 2 * (SHIFTS - 1) + (ns - 1))

    def ask_z(to, frm):
        return pltpu.make_async_remote_copy(
            ask0.at[at(to, nw)], ask1.at[at(frm, nw)], az_s.at[to], az_r.at[frm],
            device_id=along.z_dev(to), device_id_type=MESH,
        )

    def ask_w(to, frm):
        return pltpu.make_async_remote_copy(
            ask2.at[at(to, nz)], ask3.at[at(frm, nz)], aw_s.at[to], aw_r.at[frm],
            device_id=along.w_dev(to), device_id_type=MESH,
        )

    def shift(k, side):
        own, held = ((pb, ps), (qb, qs))[side]
        return pltpu.make_async_remote_copy(
            own if k == 0 else held.at[k - 1],
            held.at[k],
            sh_s.at[side, k],
            sh_r.at[side, k],
            device_id=(dp_at(1 - 2 * side), sub),
            device_id_type=MESH,
        )

    along.each_z(lambda t: ask_z(t, z).start())
    shift(0, 0).start()
    unit(q_ref, qb, qlen)
    shift(0, 1).start()
    ask1[at(z, nw), :] = ask0[at(z, nw), :]

    def logits(held):
        def body(i, total):
            cols = at(i, WIDE)
            return total + mm_nt(qb[:, cols], held[:, cols])

        return SHARPNESS * lax.fori_loop(0, wides, body, jnp.zeros((rows, rows), F32), unroll=True)

    along.each_z(lambda t: ask_z(z, t).wait_recv())
    ask2[...] = mm(swap[...], ask1[...].astype(BF16))
    along.each_w(lambda t: ask_w(t, w).start())
    ask3[at(w, nz), :] = ask2[at(w, nz), :]
    first = logits(pb)
    power[0] = jnp.exp(first)
    lane = lax.broadcasted_iota(jnp.int32, (rows, rows), 1)
    row = lax.broadcasted_iota(jnp.int32, (rows, rows), 0)
    eye = jnp.where(lane == row, 1.0, 0.0).astype(F32)
    diagonal = jnp.sum(first * eye, axis=1, keepdims=True)
    along.each_w(lambda t: ask_w(w, t).wait_recv())
    asked = mm(expand[...], ask3[...].astype(BF16))
    asked = jnp.sum(asked * column[...], axis=1, keepdims=True)
    picked = jnp.where(
        asked == lax.broadcasted_iota(jnp.int32, (slots, rows), 1).astype(F32), 1.0, 0.0
    ).astype(F32)
    pick[...] = picked.astype(BF16)
    pick_t[...] = picked.T.astype(BF16)

    half_tiles = tiles // 2

    def gather_rows(i, n):
        cols = at(i, TILE)
        x1[:, cols] = mm(pick[...], pb[:, cols]).astype(BF16)
        return n

    lax.fori_loop(0, half_tiles, gather_rows, 0)
    ex[0].start_left()
    lax.fori_loop(half_tiles, tiles, gather_rows, 0)
    ex[0].start_right()

    slot = lax.broadcasted_iota(jnp.int32, (rows, slots), 1)
    chosen = jnp.zeros((rows, slots), F32)
    for n in range(neg_ref.shape[1]):
        chosen = chosen + jnp.where(neg_ref[:, n : n + 1] == slot, 1.0, 0.0)
    limits = jnp.broadcast_to(cnt_ref[...].astype(F32), (8, ndp)).astype(BF16)
    live = jnp.where(place[...] < mm(limits, spread[...]), 1.0, 0.0)
    gq[:, pl.ds(0, slots)] = chosen * live[0:1]

    for side in range(2):
        shift(0, side).wait_recv()
        shift(1, side).start()
    power[1] = jnp.exp(logits(ps.at[0]))
    ex[0].turn_left()
    for side in range(2):
        shift(1, side).wait_recv()
        shift(2, side).start()
    power[2] = jnp.exp(logits(ps.at[1]))
    ex[0].turn_right()
    ex[0].end_left()

    def hard_logits(i, total):
        cols = at(i, depth // 4)
        return total + mm_nt(qb[:, cols], y1[:, cols])

    hard = lax.fori_loop(0, 2, hard_logits, jnp.zeros((rows, slots), F32), unroll=True)
    ex[0].end_right()
    hard = lax.fori_loop(2, 4, hard_logits, hard, unroll=True)
    hard = jnp.exp(SHARPNESS * hard) * gq[:, pl.ds(0, slots)]
    shift(2, 0).wait_recv()
    power[3] = jnp.exp(logits(ps.at[2]))
    totals = jnp.sum(hard, axis=1, keepdims=True)
    for k in range(SHIFTS):
        totals = totals + jnp.sum(power[k], axis=1, keepdims=True)
    hard = hard / totals
    hard_w[...] = hard.astype(BF16)
    hard_t = hard.T.astype(BF16)

    def slot_sums(i, n):
        cols = at(i, TILE)
        x2[:, cols] = (SHARPNESS * mm(hard_t, qb[:, cols])).astype(BF16)
        return n

    lax.fori_loop(0, half_tiles, slot_sums, 0, unroll=True)
    ex[1].start_left()
    lax.fori_loop(half_tiles, tiles, slot_sums, 0, unroll=True)
    ex[1].start_right()

    def wt_copy(k):
        return pltpu.make_async_remote_copy(
            wt.at[k], wt_in.at[k - 1], wt_s.at[k - 1], wt_r.at[k - 1],
            device_id=(dp_at(-k), sub), device_id_type=MESH,
        )

    for k in range(SHIFTS):
        weight = power[k] / totals
        if k == 0:
            weight = weight - eye
        wrow[k] = weight.astype(BF16)
        wt[k] = weight.T.astype(BF16)
        if k:
            wt_copy(k).start()

    part = jnp.sum(jnp.log(totals) - diagonal)

    def lz(to, frm):
        return pltpu.make_async_remote_copy(
            l1.at[z], l1.at[frm], lz_s.at[to], lz_r.at[frm],
            device_id=along.z_dev(to), device_id_type=MESH,
        )

    def lw(to, frm):
        return pltpu.make_async_remote_copy(
            l2.at[w], l2.at[frm], lw_s.at[to], lw_r.at[frm],
            device_id=along.w_dev(to), device_id_type=MESH,
        )

    def lsub(to, frm):
        return pltpu.make_async_remote_copy(
            l3.at[sub], l3.at[frm], lsub_s.at[to], lsub_r.at[frm],
            device_id=(me, to), device_id_type=MESH,
        )

    def ordered_sum(ref):
        total = ref[0]
        for i in range(1, ref.shape[0]):
            total = total + ref[i]
        return total

    l1[pl.ds(z, 1)] = jnp.broadcast_to(part, (1, 8, 128))
    along.each_z(lambda t: lz(t, z).start())

    def project(raw, length, grad, out):
        size = length[...]

        def radial(i, total):
            cols = at(i, WIDE)
            return total + jnp.sum(
                raw[:, cols].astype(F32) / size * grad[:, cols], axis=1, keepdims=True
            )

        along_unit = lax.fori_loop(0, wides, radial, jnp.zeros((rows, 1), F32), unroll=True)

        def write(i, n):
            cols = at(i, WIDE)
            u = raw[:, cols].astype(F32) / size
            out[:, cols] = ((grad[:, cols] - u * along_unit) / size).astype(BF16)
            return n

        lax.fori_loop(0, wides, write, 0)

    def query_side(i, n):
        cols = at(i, WIDE)
        total = mm(hard_w[...], y1[:, cols]) + mm(wrow[0], pb[:, cols])
        for k in range(1, SHIFTS):
            total = total + mm(wrow[k], ps[k - 1, :, cols])
        gq[:, cols] = SHARPNESS * total
        return n

    lax.fori_loop(0, wides, query_side, 0)

    along.each_z(lambda t: lz(z, t).wait_recv())
    l2[pl.ds(w, 1)] = ordered_sum(l1)[None]
    along.each_w(lambda t: lw(t, w).start())

    project(q_ref, qlen, gq, dq_ref)

    for k in range(1, SHIFTS):
        wt_copy(k).wait_recv()
    shift(2, 1).wait_recv()

    def passage_side(i, n):
        cols = at(i, WIDE)
        total = mm(wt[0], qb[:, cols])
        for k in range(1, SHIFTS):
            total = total + mm(wt_in[k - 1], qs[k - 1, :, cols])
        gp[:, cols] = SHARPNESS * total
        return n

    lax.fori_loop(0, wides, passage_side, 0)
    ex[1].turn_left()
    ex[1].turn_right()

    along.each_w(lambda t: lw(w, t).wait_recv())
    l3[pl.ds(sub, 1)] = ordered_sum(l2)[None]
    each_sub(lambda t: lsub(t, sub).start())


    each_sub(lambda t: lsub(sub, t).wait_recv())
    loss_ref[...] = (ordered_sum(l3) / float(rows * ndp * ns))[0:1, 0:1]

    def add_returned(i, n):
        cols = at(i, TILE)
        gp[:, cols] = gp[:, cols] + mm(pick_t[...], y2[:, cols])
        return n

    ex[1].end_left()
    lax.fori_loop(0, half_tiles, add_returned, 0, unroll=True)
    ex[1].end_right()
    lax.fori_loop(half_tiles, tiles, add_returned, 0, unroll=True)
    project(p_ref, plen, gp, dp_ref)

    along.each_z(lambda t: ask_z(t, z).wait_send())
    along.each_w(lambda t: ask_w(t, w).wait_send())
    for k in range(SHIFTS - 1):
        for side in range(2):
            shift(k, side).wait_send()
    for k in range(1, SHIFTS):
        wt_copy(k).wait_send()
    along.each_z(lambda t: lz(t, z).wait_send())
    along.each_w(lambda t: lw(t, w).wait_send())
    each_sub(lambda t: lsub(t, sub).wait_send())
    for e in ex:
        e.drain()


def on_device(nz, nw, ns, queries, passages, requests, counts, neg_slot):
    rows, depth = queries.shape
    ndp = nz * nw
    slots = ndp * CAP
    half, quarter = depth // 2, depth // 4
    dma = pltpu.SemaphoreType.DMA
    v = pltpu.VMEM
    wide = lambda: [
        v((slots, half), BF16),
        v((2 * slots, quarter), BF16),
        v((2 * slots, quarter), BF16),
        v((2 * slots, quarter), BF16),
        v((2 * slots, quarter), BF16),
        v((2 * slots, quarter), BF16),
    ]
    n = SHIFTS - 1
    scratch = (
        [v((ndp, 128), F32)] * 4
        + [v((rows, depth), BF16)] * 2
        + [v((rows, 1), F32)] * 2
        + [v((n, rows, depth), BF16)] * 2
        + [v((slots, depth), BF16)] * 4
        + [wide(), wide()]
        + [v((SHIFTS, rows, rows), F32)]
        + [v((SHIFTS, rows, rows), BF16)] * 2
        + [v((n, rows, rows), BF16)]
        + [v((rows, slots), BF16), v((slots, rows), BF16), v((rows, slots), BF16)]
        + [v((rows, depth), F32)] * 2
        + [v((nz, 8, 128), F32), v((nw, 8, 128), F32), v((ns, 8, 128), F32)]
        + [dma((nz,)), dma((nz,)), dma((nw,)), dma((nw,))]
        + [dma((2, n)), dma((2, n))]
        + [dma((2, 3, nz)), dma((2, 3, nz)), dma((2, 2, nw)), dma((2, 2, nw)), dma((2, 5))]
        + [dma((n,)), dma((n,))]
        + [dma((nz,)), dma((nz,)), dma((nw,)), dma((nw,)), dma((ns,)), dma((ns,))]

    )
    vmem = pl.BlockSpec(memory_space=pltpu.VMEM)
    fixed = tables(nz, nw)
    flops = 2 * rows * depth * (SHIFTS * rows * 3 + slots * 5) + 14 * slots * slots * depth
    dq, dp, loss = pl.pallas_call(
        functools.partial(kernel, nz, nw, ns),
        out_shape=(
            jax.ShapeDtypeStruct((rows, depth), BF16),
            jax.ShapeDtypeStruct((rows, depth), BF16),
            jax.ShapeDtypeStruct((1, 1), F32),
        ),
        in_specs=[vmem] * (5 + len(fixed)),
        out_specs=(vmem, vmem, vmem),
        scratch_shapes=scratch,
        compiler_params=pltpu.CompilerParams(
            collective_id=0, has_side_effects=True, vmem_limit_bytes=60 << 20
        ),
        cost_estimate=pl.CostEstimate(
            flops=flops, bytes_accessed=12 * rows * depth, transcendentals=rows * slots * 2
        ),
    )(queries, passages, requests, counts, neg_slot, *fixed)
    return dq, dp, loss.reshape(())


def solution(mesh):
    ndp, ns = mesh.shape["dp"], mesh.shape["sub"]
    nz = Z_SIZE
    placed = (
        P(("dp", "sub"), None),
        P(("dp", "sub"), None),
        P(("dp", "sub"), None, None),
        P(("dp", "sub"), None),
        P(("dp", "sub"), None),
    )
    return jax.shard_map(
        functools.partial(on_device, nz, ndp // nz, ns),
        mesh=mesh,
        in_specs=placed,
        out_specs=(P(("dp", "sub"), None), P(("dp", "sub"), None), P()),
        check_vma=False,
    )
```
